32 devices in a mesh: ctx: 4 (over z), head: 2 (over x), rep: 4 (over y, core).
Axes of the slice: x: 2, y: 2, z: 4, core: 2. Of those that a mesh axis runs over, the one named last changes fastest.
Arguments:
- trunk_query_array: bfloat16 [2048, 8192], P(('rep', 'ctx'), 'head'), parts along dimension 0, may hold values from -200 to 200
- trunk_key_array: bfloat16 [2048, 1024], P(('rep', 'ctx'), 'head'), parts along dimension 0, may hold values from -6 to 6
- trunk_value_array: bfloat16 [2048, 1024], P(('rep', 'ctx'), 'head'), parts along dimension 0, may hold values from -15 to 15
- tree_query_array: bfloat16 [40960, 8192], P(('rep', 'ctx'), 'head'), parts along dimension 0, may hold values from -200 to 200
- tree_key_array: bfloat16 [40960, 1024], P(('rep', 'ctx'), 'head'), parts along dimension 0, may hold values from -6 to 6
- tree_value_array: bfloat16 [40960, 1024], P(('rep', 'ctx'), 'head'), parts along dimension 0, may hold values from -15 to 15
- ancestors: int32 [320, 2], P('rep'), parts along dimension 0, may hold values from -1 to 79, as said below
Outputs:
- trunk_out: bfloat16 [2048, 8192], P(('rep', 'ctx'), 'head'), parts along dimension 0
- tree_out: bfloat16 [40960, 8192], P(('rep', 'ctx'), 'head'), parts along dimension 0
The draws below stay inside these ranges and needn't reach their ends.
There are 4 independent parts, one for each index of `rep`. The reference program is written for one: setup_inputs(seed, part) draws one part's arguments, and reference() takes and returns one part's arrays. A program takes and returns all parts, laid end to end along the dimension named above; each array names one. Nothing has to cross between parts.
Inputs may be any that keep to these rules, and one draw needn't show every extreme that they name: `ancestors`: row s holds the slot of the grandparent and of the parent of the segment in slot s, -1 where there is none. The segments form a tree: 16 segments below the trunk, 2 children under each, 1 leaf child under each of those; slots 20 * c to 20 * c + 19 lie on index c of ctx, and the segments are placed on slots in any order, except that slot 79 always holds a segment that has children. No index of ctx holds more than 16 segments that have children, and some index holds exactly 16.
All inputs are finite; a program needn't handle non-finite values.
Results may differ from the reference program's by a relative error of at most 0.0045.
Values may be sent and summed in bfloat16 or wider, within the bound.
A program may use at most 320 MiB of HBM per device.

```python
import math
import jax
import jax.numpy as jnp
from jax import lax

QUERY_HEADS = 64
KEY_VALUE_HEADS = 8
HEAD_SIZE = 128
SEGMENT_TOKENS = 128
TRUNK_PER_PART = 128
FAN1 = 16
FAN2 = 2
FAN3 = 1
SEGMENT_TOTAL = 80
TRUNK_TOKENS = 512
N_CTX = 4


def trunk_key_table(key):
    block_width = KEY_VALUE_HEADS * HEAD_SIZE
    base_table = jnp.clip(jax.random.normal(jax.random.fold_in(key, 101), (TRUNK_TOKENS, block_width), jnp.float32), -6.0, 6.0)
    return base_table


def query_table(key, salt, row_total):
    block_width = QUERY_HEADS * HEAD_SIZE
    table = jnp.clip(2.0 * jax.random.normal(jax.random.fold_in(key, salt), (row_total, block_width), jnp.float32), -12.0, 12.0)
    return table.astype(jnp.bfloat16)


def draw_trunk_key_array(key, part):
    keys_table = trunk_key_table(key)
    return keys_table.astype(jnp.bfloat16)


def draw_trunk_query_array(key, part):
    return query_table(key, 201, TRUNK_TOKENS)


def draw_tree_query_array(key, part):
    return query_table(key, 301, SEGMENT_TOTAL * SEGMENT_TOKENS)


def draw_ancestors(key, part):
    members = N_CTX
    slot_count = SEGMENT_TOTAL // members
    inner_total = FAN1 + FAN1 * FAN2
    leaf_total = SEGMENT_TOTAL - inner_total
    average = inner_total // members
    excess = max(1, average // 3)
    paired = 2 * (members // 4)
    device_order = jax.random.permutation(jax.random.fold_in(key, 401), members)
    placed = jnp.argsort(device_order)
    shift_by = jnp.where(placed < paired, jnp.where(placed % 2 == 0, excess, -excess), 0)
    counts = average + shift_by
    counts = counts.at[members - 1].set(jnp.maximum(counts[members - 1], 1))
    counts = counts.at[members - 2].set(inner_total - jnp.sum(counts) + counts[members - 2])
    subkeys = jax.random.split(jax.random.fold_in(key, 402), members)
    local_rank = jax.vmap(lambda subkey: jax.random.permutation(subkey, slot_count))(subkeys)
    last_row = (local_rank[members - 1] - local_rank[members - 1, slot_count - 1]) % slot_count
    local_rank = local_rank.at[members - 1].set(last_row)
    inner_slot = (local_rank < counts[:, None]).reshape(-1)
    slot_index = jnp.arange(SEGMENT_TOTAL, dtype=jnp.int32)
    listing = jnp.argsort(jnp.where(inner_slot, 0, SEGMENT_TOTAL) + slot_index).astype(jnp.int32)
    inner_order = jax.random.permutation(jax.random.fold_in(key, 403), inner_total)
    leaf_order = inner_total + jax.random.permutation(jax.random.fold_in(key, 404), leaf_total)
    segment_at = jnp.concatenate([inner_order, leaf_order]).astype(jnp.int32)
    slot_of_segment = jnp.zeros((SEGMENT_TOTAL,), jnp.int32).at[segment_at].set(listing)
    segment_of_slot = jnp.zeros((SEGMENT_TOTAL,), jnp.int32).at[listing].set(segment_at)

    def parent_of(segment):
        second_level = segment >= FAN1
        leaf_level = segment >= inner_total
        return jnp.where(leaf_level, FAN1 + (segment - inner_total) // FAN3, jnp.where(second_level, (segment - FAN1) // FAN2, -1))
    parent = parent_of(segment_of_slot)
    grandparent = jnp.where(parent >= 0, parent_of(jnp.maximum(parent, 0)), -1)
    parent_slot = jnp.where(parent >= 0, slot_of_segment[jnp.maximum(parent, 0)], -1)
    grand_slot = jnp.where(grandparent >= 0, slot_of_segment[jnp.maximum(grandparent, 0)], -1)
    return jnp.stack([grand_slot, parent_slot], axis=1).astype(jnp.int32)


def level_of(stream_key, dims, pieces, least, largest):
    def one(dim, shards_of):
        heights = jax.random.uniform(jax.random.fold_in(jax.random.fold_in(stream_key, 6), dim), (shards_of,), jnp.float32, least / len(pieces), largest / len(pieces))
        return jnp.repeat(jnp.exp(heights), dims[dim] // shards_of).reshape((-1,) + (1,) * (len(dims) - dim - 1))

    factor_of = one(*pieces[0])
    for cut in pieces[1:]:
        factor_of = factor_of * one(*cut)
    return factor_of


def bell_draw(key, extent, spread, bound, pieces=(), held_as=jnp.bfloat16):
    drawn = jax.random.normal(key, extent, jnp.float32) * spread
    if len(pieces) > 0:
        drawn = level_of(key, extent, pieces, -0.22, 0.18) * drawn
    return jnp.clip(drawn, min=-bound, max=bound).astype(held_as)


def setup_inputs(seed: int = 0, part: int = 0) -> dict:
    key_of = jax.random.split(jax.random.key(seed), 8)
    part_keys = jax.random.split(jax.random.fold_in(key_of[7], part), 8)
    return {
        "trunk_query_array": draw_trunk_query_array(jax.random.fold_in(jax.random.fold_in(key_of[7], part), 71), part),
        "trunk_key_array": draw_trunk_key_array(jax.random.fold_in(jax.random.fold_in(key_of[7], part), 71), part),
        "trunk_value_array": bell_draw(part_keys[2], (TRUNK_TOKENS, KEY_VALUE_HEADS * HEAD_SIZE), 3.0, 15.0, ((0, 4), (1, 2))),
        "tree_query_array": draw_tree_query_array(jax.random.fold_in(jax.random.fold_in(key_of[7], part), 71), part),
        "tree_key_array": bell_draw(part_keys[4], (SEGMENT_TOTAL * SEGMENT_TOKENS, KEY_VALUE_HEADS * HEAD_SIZE), 1.0, 6.0, ((0, 4), (1, 2))),
        "tree_value_array": bell_draw(part_keys[5], (SEGMENT_TOTAL * SEGMENT_TOKENS, KEY_VALUE_HEADS * HEAD_SIZE), 3.0, 15.0, ((0, 4), (1, 2))),
        "ancestors": draw_ancestors(jax.random.fold_in(jax.random.fold_in(key_of[7], part), 71), part),
    }


masked_score = -1e+30

def attend(queries, key_rows, value_rows, allowed):
    inverse_root = 1.0 / math.sqrt(HEAD_SIZE)
    scores = jnp.einsum('rhgd,khd->rhgk', queries.astype(jnp.float32), key_rows.astype(jnp.float32)) * inverse_root
    allowed_full = allowed[:, None, None, :]
    scores = jnp.where(allowed_full, scores, masked_score)
    peak = lax.optimization_barrier(jnp.max(scores, axis=-1, keepdims=True))
    weights = jnp.where(allowed_full, jnp.exp(scores - peak), 0.0)
    totals = lax.optimization_barrier(jnp.sum(weights, axis=-1))
    rounded = lax.optimization_barrier(weights.astype(jnp.bfloat16))
    weighted = jnp.einsum('rhgk,khd->rhgd', rounded.astype(jnp.float32), value_rows.astype(jnp.float32))
    return (weighted / totals[..., None]).astype(jnp.bfloat16)

def reference(trunk_query_array, trunk_key_array, trunk_value_array, tree_query_array, tree_key_array, tree_value_array, ancestors):
    query_group_size = QUERY_HEADS // KEY_VALUE_HEADS
    trunk_key_rows = trunk_key_array.reshape(TRUNK_TOKENS, KEY_VALUE_HEADS, HEAD_SIZE)
    trunk_value_rows = trunk_value_array.reshape(TRUNK_TOKENS, KEY_VALUE_HEADS, HEAD_SIZE)
    tree_key_rows = tree_key_array.reshape(SEGMENT_TOTAL, SEGMENT_TOKENS, KEY_VALUE_HEADS, HEAD_SIZE)
    tree_value_rows = tree_value_array.reshape(SEGMENT_TOTAL, SEGMENT_TOKENS, KEY_VALUE_HEADS, HEAD_SIZE)
    key_positions = jnp.arange(TRUNK_TOKENS, dtype=jnp.int32)
    trunk_block_list = trunk_query_array.reshape(N_CTX, TRUNK_PER_PART, KEY_VALUE_HEADS, query_group_size, HEAD_SIZE)

    def trunk_step(inputs):
        block_index, queries = inputs
        positions = block_index * TRUNK_PER_PART + jnp.arange(TRUNK_PER_PART, dtype=jnp.int32)
        allowed = positions[:, None] >= key_positions[None, :]
        return attend(queries, trunk_key_rows, trunk_value_rows, allowed)
    trunk_out = lax.map(trunk_step, (jnp.arange(N_CTX, dtype=jnp.int32), trunk_block_list))
    trunk_out = trunk_out.reshape(TRUNK_TOKENS, QUERY_HEADS * HEAD_SIZE)
    tree_block_list = tree_query_array.reshape(SEGMENT_TOTAL, SEGMENT_TOKENS, KEY_VALUE_HEADS, query_group_size, HEAD_SIZE)
    offsets = jnp.arange(SEGMENT_TOKENS, dtype=jnp.int32)
    causal = offsets[:, None] >= offsets[None, :]

    def tree_step(inputs):
        slot_number, queries = inputs
        parents = ancestors[slot_number]
        picked_rows = jnp.maximum(parents, 0).astype(jnp.int32)
        key_rows = jnp.concatenate([trunk_key_rows, tree_key_rows[picked_rows].reshape(2 * SEGMENT_TOKENS, KEY_VALUE_HEADS, HEAD_SIZE), tree_key_rows[slot_number]], axis=0)
        value_rows = jnp.concatenate([trunk_value_rows, tree_value_rows[picked_rows].reshape(2 * SEGMENT_TOKENS, KEY_VALUE_HEADS, HEAD_SIZE), tree_value_rows[slot_number]], axis=0)
        first_seen = jnp.broadcast_to(parents[0] >= 0, (SEGMENT_TOKENS, SEGMENT_TOKENS))
        second_seen = jnp.broadcast_to(parents[1] >= 0, (SEGMENT_TOKENS, SEGMENT_TOKENS))
        allowed = jnp.concatenate([jnp.ones((SEGMENT_TOKENS, TRUNK_TOKENS), dtype=bool), first_seen, second_seen, causal], axis=1)
        return attend(queries, key_rows, value_rows, allowed)
    tree_out = lax.map(tree_step, (jnp.arange(SEGMENT_TOTAL, dtype=jnp.int32), tree_block_list))
    tree_out = tree_out.reshape(SEGMENT_TOTAL * SEGMENT_TOKENS, QUERY_HEADS * HEAD_SIZE)
    return (trunk_out, tree_out)
```

```python
import functools
import math

import jax
import jax.numpy as jnp
from jax import lax
from jax.experimental import pallas as pl
from jax.experimental.pallas import tpu as pltpu
from jax.sharding import PartitionSpec as P

HEAD_SIZE = 128
SEGMENT_TOKENS = 128
GROUP = 8
ROW_HEADS = 2
STAT_HALF = 64
MASKED = -1e30
LOG2E_SCALE = math.log2(math.e) / math.sqrt(HEAD_SIZE)


def stack_heads(ref, first, count):
    blocks = [
        ref[:, (first + h) * HEAD_SIZE : (first + h + 1) * HEAD_SIZE] for h in range(count)
    ]
    return jnp.concatenate(blocks, axis=0)


def scores_of(queries, key_rows):
    return lax.dot_general(
        queries, key_rows, (((1,), (1,)), ((), ())), preferred_element_type=jnp.float32
    )


def with_ones(value_rows):
    return jnp.concatenate([value_rows, jnp.ones_like(value_rows)], axis=1)


def head_cols(ref, j):
    return ref[:, j * HEAD_SIZE : (j + 1) * HEAD_SIZE]


def near_kernel(kv_heads, q_ref, kt_ref, vt_ref, ks_ref, vs_ref, o_ref, stat_ref):
    rows = ROW_HEADS * SEGMENT_TOKENS
    lane = lax.broadcasted_iota(jnp.int32, (SEGMENT_TOKENS, 2 * STAT_HALF), 1)
    query_at = lax.broadcasted_iota(jnp.int32, (rows, SEGMENT_TOKENS), 0) % SEGMENT_TOKENS
    key_at = lax.broadcasted_iota(jnp.int32, (rows, SEGMENT_TOKENS), 1)
    causal = query_at >= key_at
    stats = jnp.zeros((SEGMENT_TOKENS, 2 * STAT_HALF), jnp.float32)
    for j in range(kv_heads):
        trunk_keys, self_keys = head_cols(kt_ref, j), head_cols(ks_ref, j)
        trunk_values = with_ones(head_cols(vt_ref, j))
        self_values = with_ones(head_cols(vs_ref, j))
        for first in range(j * GROUP, (j + 1) * GROUP, ROW_HEADS):
            queries = stack_heads(q_ref, first, ROW_HEADS)
            trunk_scores = scores_of(queries, trunk_keys)
            self_scores = jnp.where(causal, scores_of(queries, self_keys), MASKED)
            peak = jnp.maximum(
                jnp.max(trunk_scores, axis=1, keepdims=True),
                jnp.max(self_scores, axis=1, keepdims=True),
            )
            trunk_weights = jnp.exp2((trunk_scores - peak) * LOG2E_SCALE).astype(jnp.bfloat16)
            self_weights = jnp.exp2((self_scores - peak) * LOG2E_SCALE).astype(jnp.bfloat16)
            summed = jnp.dot(
                trunk_weights, trunk_values, preferred_element_type=jnp.float32
            ) + jnp.dot(self_weights, self_values, preferred_element_type=jnp.float32)
            for h in range(ROW_HEADS):
                part = slice(h * SEGMENT_TOKENS, (h + 1) * SEGMENT_TOKENS)
                head = first + h
                o_ref[:, head * HEAD_SIZE : (head + 1) * HEAD_SIZE] = summed[
                    part, :HEAD_SIZE
                ].astype(jnp.bfloat16)
                stats = jnp.where(lane == head, peak[part], stats)
                stats = jnp.where(lane == STAT_HALF + head, summed[part, HEAD_SIZE:], stats)
    stat_ref[...] = stats


def far_kernel(
    kv_heads, place_ref, seen_ref, q_ref, near_ref, stat_ref, kv0_ref, kv1_ref, o_ref
):
    step = pl.program_id(0)
    rows = ROW_HEADS * SEGMENT_TOKENS
    bars = [
        jnp.where(seen_ref[2 * step + n] > 0, 0.0, MASKED).astype(jnp.float32) for n in range(2)
    ]
    key_at = lax.broadcasted_iota(jnp.int32, (1, 2 * SEGMENT_TOKENS), 1)
    bar = jnp.where(key_at < SEGMENT_TOKENS, bars[0], bars[1])
    width = kv_heads * HEAD_SIZE
    for j in range(kv_heads):
        cols = slice(j * HEAD_SIZE, (j + 1) * HEAD_SIZE)
        vcols = slice(width + j * HEAD_SIZE, width + (j + 1) * HEAD_SIZE)
        keys = jnp.concatenate([kv0_ref[0, :, cols], kv1_ref[0, :, cols]], axis=0)
        values = with_ones(jnp.concatenate([kv0_ref[0, :, vcols], kv1_ref[0, :, vcols]], axis=0))
        for first in range(j * GROUP, (j + 1) * GROUP, ROW_HEADS):
            queries = stack_heads(q_ref, first, ROW_HEADS)
            scores = scores_of(queries, keys) + bar
            near_peak = jnp.concatenate(
                [stat_ref[:, first + h : first + h + 1] for h in range(ROW_HEADS)], axis=0
            )
            near_total = jnp.concatenate(
                [
                    stat_ref[:, STAT_HALF + first + h : STAT_HALF + first + h + 1]
                    for h in range(ROW_HEADS)
                ],
                axis=0,
            )
            peak = jnp.maximum(near_peak, jnp.max(scores, axis=1, keepdims=True))
            weights = jnp.exp2((scores - peak) * LOG2E_SCALE).astype(jnp.bfloat16)
            summed = jnp.dot(weights, values, preferred_element_type=jnp.float32)
            factor = jnp.exp2((near_peak - peak) * LOG2E_SCALE)
            near = stack_heads(near_ref, first, ROW_HEADS).astype(jnp.float32)
            total = factor * near_total + summed[:, HEAD_SIZE:]
            out = ((factor * near + summed[:, :HEAD_SIZE]) / total).astype(jnp.bfloat16)
            for h in range(ROW_HEADS):
                part = slice(h * SEGMENT_TOKENS, (h + 1) * SEGMENT_TOKENS)
                head = first + h
                o_ref[:, head * HEAD_SIZE : (head + 1) * HEAD_SIZE] = out[part]


def trunk_kernel(kv_heads, start_ref, q_ref, kt_ref, vt_ref, o_ref):
    rows = q_ref.shape[0]
    key_count = kt_ref.shape[0]
    query_at = start_ref[0] + lax.broadcasted_iota(jnp.int32, (rows, key_count), 0)
    causal = query_at >= lax.broadcasted_iota(jnp.int32, (rows, key_count), 1)
    for j in range(kv_heads):
        keys = head_cols(kt_ref, j)
        values = with_ones(head_cols(vt_ref, j))
        for head in range(j * GROUP, (j + 1) * GROUP):
            scores = jnp.where(causal, scores_of(head_cols(q_ref, head), keys), MASKED)
            peak = jnp.max(scores, axis=1, keepdims=True)
            weights = jnp.exp2((scores - peak) * LOG2E_SCALE).astype(jnp.bfloat16)
            summed = jnp.dot(weights, values, preferred_element_type=jnp.float32)
            o_ref[:, head * HEAD_SIZE : (head + 1) * HEAD_SIZE] = (
                summed[:, :HEAD_SIZE] / summed[:, HEAD_SIZE:]
            ).astype(jnp.bfloat16)


VMEM_LIMIT = 48 * 1024 * 1024


def near_call(tree_query, key_all, value_all, tree_key, tree_value):
    tokens, width = tree_query.shape
    slots = tokens // SEGMENT_TOKENS
    kv_width = tree_key.shape[1]
    kv_heads = kv_width // HEAD_SIZE
    trunk = key_all.shape[0]
    keys = trunk + SEGMENT_TOKENS
    whole = pl.BlockSpec((trunk, kv_width), lambda s: (0, 0))
    own = pl.BlockSpec((SEGMENT_TOKENS, kv_width), lambda s: (s, 0))
    wide = pl.BlockSpec((SEGMENT_TOKENS, width), lambda s: (s, 0))
    return pl.pallas_call(
        functools.partial(near_kernel, kv_heads),
        grid=(slots,),
        in_specs=[wide, whole, whole, own, own],
        out_specs=[wide, pl.BlockSpec((SEGMENT_TOKENS, 2 * STAT_HALF), lambda s: (s, 0))],
        out_shape=[
            jax.ShapeDtypeStruct((tokens, width), jnp.bfloat16),
            jax.ShapeDtypeStruct((tokens, 2 * STAT_HALF), jnp.float32),
        ],
        compiler_params=pltpu.CompilerParams(vmem_limit_bytes=VMEM_LIMIT),
        cost_estimate=pl.CostEstimate(
            flops=4 * tokens * width * keys,
            bytes_accessed=4 * tokens * width,
            transcendentals=tokens * width // HEAD_SIZE * keys,
        ),
        name="near",
    )(tree_query, key_all, value_all, tree_key, tree_value)


def far_call(places, seen, tree_query, near, stats, gathered):
    tokens, width = tree_query.shape
    slots = tokens // SEGMENT_TOKENS
    kv_width = gathered.shape[2]
    kv_heads = kv_width // HEAD_SIZE // 2
    wide = pl.BlockSpec((SEGMENT_TOKENS, width), lambda s, p, v: (s, 0))
    return pl.pallas_call(
        functools.partial(far_kernel, kv_heads),
        grid_spec=pltpu.PrefetchScalarGridSpec(
            num_scalar_prefetch=2,
            grid=(slots,),
            in_specs=[
                wide,
                wide,
                pl.BlockSpec((SEGMENT_TOKENS, 2 * STAT_HALF), lambda s, p, v: (s, 0)),
                pl.BlockSpec((1, SEGMENT_TOKENS, kv_width), lambda s, p, v: (p[2 * s], 0, 0)),
                pl.BlockSpec((1, SEGMENT_TOKENS, kv_width), lambda s, p, v: (p[2 * s + 1], 0, 0)),
            ],
            out_specs=wide,
        ),
        out_shape=jax.ShapeDtypeStruct((tokens, width), jnp.bfloat16),
        compiler_params=pltpu.CompilerParams(vmem_limit_bytes=VMEM_LIMIT),
        cost_estimate=pl.CostEstimate(
            flops=8 * tokens * width * SEGMENT_TOKENS,
            bytes_accessed=6 * tokens * width,
            transcendentals=tokens * width * 2,
        ),
        name="far",
    )(places, seen, tree_query, near, stats, gathered, gathered)


def trunk_call(start, trunk_query, key_all, value_all):
    rows, width = trunk_query.shape
    kv_heads = key_all.shape[1] // HEAD_SIZE
    vmem = pl.BlockSpec(memory_space=pltpu.VMEM)
    return pl.pallas_call(
        functools.partial(trunk_kernel, kv_heads),
        in_specs=[pl.BlockSpec(memory_space=pltpu.SMEM), vmem, vmem, vmem],
        out_specs=vmem,
        out_shape=jax.ShapeDtypeStruct((rows, width), jnp.bfloat16),
        compiler_params=pltpu.CompilerParams(vmem_limit_bytes=VMEM_LIMIT),
        cost_estimate=pl.CostEstimate(
            flops=4 * rows * width * key_all.shape[0],
            bytes_accessed=4 * rows * width,
            transcendentals=rows * width // HEAD_SIZE * key_all.shape[0],
        ),
        name="trunk",
    )(start, trunk_query, key_all, value_all)


def local(
    trunk_query,
    trunk_key,
    trunk_value,
    tree_query,
    tree_key,
    tree_value,
    ancestors,
):
    me = lax.axis_index("ctx")
    kv_width = trunk_key.shape[1]
    slots = tree_query.shape[0] // SEGMENT_TOKENS
    total = ancestors.shape[0]
    sent = slots * 4 // 5

    slot_ids = jnp.arange(total, dtype=jnp.int32)
    inner = jnp.any(ancestors.reshape(-1, 1) == slot_ids[None, :], axis=0)
    earlier = (slot_ids[None, :] < slot_ids[:, None]) & (
        slot_ids[None, :] // slots == slot_ids[:, None] // slots
    )
    rank = jnp.sum(jnp.where(earlier & inner[None, :], 1, 0), axis=1)
    place = slot_ids // slots * sent + rank
    own_place = me * sent + jnp.arange(sent, dtype=jnp.int32)
    hit = inner[None, :] & (place[None, :] == own_place[:, None])
    picked = jnp.sum(jnp.where(hit, slot_ids[None, :] % slots, 0), axis=1)

    own_lists = lax.dynamic_slice_in_dim(ancestors, me * slots, slots, 0).reshape(-1)
    seen = (own_lists >= 0).astype(jnp.int32)
    places = jnp.sum(
        jnp.where(own_lists[:, None] == slot_ids[None, :], place[None, :], 0), axis=1
    )

    trunk_both = lax.all_gather(
        jnp.concatenate([trunk_key, trunk_value], axis=1), "ctx", axis=0, tiled=True
    )
    key_all, value_all = trunk_both[:, :kv_width], trunk_both[:, kv_width:]
    packed = jnp.concatenate(
        [
            tree_key.reshape(slots, SEGMENT_TOKENS, kv_width)[picked],
            tree_value.reshape(slots, SEGMENT_TOKENS, kv_width)[picked],
        ],
        axis=2,
    )
    gathered = lax.all_gather(packed, "ctx", axis=0, tiled=True)

    near, stats = near_call(tree_query, key_all, value_all, tree_key, tree_value)
    start = (me * trunk_query.shape[0]).astype(jnp.int32).reshape(1)
    trunk_out = trunk_call(start, trunk_query, key_all, value_all)
    tree_out = far_call(places, seen, tree_query, near, stats, gathered)
    return trunk_out, tree_out


def solution(mesh):
    split = P(("rep", "ctx"), "head")
    return jax.shard_map(
        local,
        mesh=mesh,
        in_specs=(split,) * 6 + (P("rep", None),),
        out_specs=(split, split),
        check_vma=False,
    )
```

```python
import functools
import math

import jax
import jax.numpy as jnp
from jax import lax
from jax.experimental import pallas as pl
from jax.experimental.pallas import tpu as pltpu
from jax.sharding import PartitionSpec as P

HEAD_SIZE = 128
SEGMENT_TOKENS = 128
GROUP = 8
ROW_HEADS = 2
STAT_WIDTH = 128
MASKED = -1e30
LOG2E_SCALE = math.log2(math.e) / math.sqrt(HEAD_SIZE)


def stack_heads(ref, first, count):
    blocks = [
        ref[:, (first + h) * HEAD_SIZE : (first + h + 1) * HEAD_SIZE] for h in range(count)
    ]
    return jnp.concatenate(blocks, axis=0)


def scores_of(queries, key_rows):
    return lax.dot_general(
        queries, key_rows, (((1,), (1,)), ((), ())), preferred_element_type=jnp.float32
    )


def with_ones(value_rows):
    return jnp.concatenate([value_rows, jnp.ones_like(value_rows)], axis=1)


def head_cols(ref, j):
    return ref[:, j * HEAD_SIZE : (j + 1) * HEAD_SIZE]


def near_kernel(kv_heads, q_ref, kt_ref, vt_ref, ks_ref, vs_ref, o_ref, stat_ref):
    rows = ROW_HEADS * SEGMENT_TOKENS
    lane = lax.broadcasted_iota(jnp.int32, (SEGMENT_TOKENS, STAT_WIDTH), 1)
    query_at = lax.broadcasted_iota(jnp.int32, (rows, SEGMENT_TOKENS), 0) % SEGMENT_TOKENS
    key_at = lax.broadcasted_iota(jnp.int32, (rows, SEGMENT_TOKENS), 1)
    causal = query_at >= key_at
    stats = jnp.zeros((SEGMENT_TOKENS, STAT_WIDTH), jnp.float32)
    for j in range(kv_heads):
        trunk_keys, self_keys = head_cols(kt_ref, j), head_cols(ks_ref, j)
        trunk_values = with_ones(head_cols(vt_ref, j))
        self_values = with_ones(head_cols(vs_ref, j))
        for first in range(j * GROUP, (j + 1) * GROUP, ROW_HEADS):
            queries = stack_heads(q_ref, first, ROW_HEADS)
            trunk_scores = scores_of(queries, trunk_keys)
            self_scores = jnp.where(causal, scores_of(queries, self_keys), MASKED)
            peak = jnp.maximum(
                jnp.max(trunk_scores, axis=1, keepdims=True),
                jnp.max(self_scores, axis=1, keepdims=True),
            )
            trunk_weights = jnp.exp2((trunk_scores - peak) * LOG2E_SCALE).astype(jnp.bfloat16)
            self_weights = jnp.exp2((self_scores - peak) * LOG2E_SCALE).astype(jnp.bfloat16)
            summed = jnp.dot(
                trunk_weights, trunk_values, preferred_element_type=jnp.float32
            ) + jnp.dot(self_weights, self_values, preferred_element_type=jnp.float32)
            for h in range(ROW_HEADS):
                part = slice(h * SEGMENT_TOKENS, (h + 1) * SEGMENT_TOKENS)
                head = first + h
                total = summed[part, HEAD_SIZE:]
                o_ref[:, head * HEAD_SIZE : (head + 1) * HEAD_SIZE] = (
                    summed[part, :HEAD_SIZE] / total
                ).astype(jnp.bfloat16)
                level = peak[part] * LOG2E_SCALE + jnp.log2(total)
                stats = jnp.where(lane == head, level, stats)
    stat_ref[...] = stats


def far_kernel(
    first_kv,
    kv_count,
    place_ref,
    seen_ref,
    q_ref,
    near_ref,
    stat_ref,
    kv0_ref,
    kv1_ref,
    *rest,
):
    o_ref = rest[-1]
    step = pl.program_id(0)
    bars = [
        jnp.where(seen_ref[2 * step + n] > 0, 0.0, MASKED).astype(jnp.float32) for n in range(2)
    ]
    key_at = lax.broadcasted_iota(jnp.int32, (1, 2 * SEGMENT_TOKENS), 1)
    bar = jnp.where(key_at < SEGMENT_TOKENS, bars[0], bars[1])
    width = kv_count * HEAD_SIZE
    for j in range(kv_count):
        cols = slice(j * HEAD_SIZE, (j + 1) * HEAD_SIZE)
        vcols = slice(width + j * HEAD_SIZE, width + (j + 1) * HEAD_SIZE)
        keys = jnp.concatenate([kv0_ref[0, :, cols], kv1_ref[0, :, cols]], axis=0)
        values = with_ones(jnp.concatenate([kv0_ref[0, :, vcols], kv1_ref[0, :, vcols]], axis=0))
        for first in range(j * GROUP, (j + 1) * GROUP, ROW_HEADS):
            queries = stack_heads(q_ref, first, ROW_HEADS)
            scores = scores_of(queries, keys) * LOG2E_SCALE + bar
            stat = first_kv * GROUP + first
            level = jnp.concatenate(
                [stat_ref[:, stat + h : stat + h + 1] for h in range(ROW_HEADS)], axis=0
            )
            peak = jnp.maximum(level, jnp.max(scores, axis=1, keepdims=True))
            weights = jnp.exp2(scores - peak).astype(jnp.bfloat16)
            summed = jnp.dot(weights, values, preferred_element_type=jnp.float32)
            factor = jnp.exp2(level - peak)
            near = stack_heads(near_ref, first, ROW_HEADS).astype(jnp.float32)
            total = factor + summed[:, HEAD_SIZE:]
            out = ((factor * near + summed[:, :HEAD_SIZE]) / total).astype(jnp.bfloat16)
            for h in range(ROW_HEADS):
                part = slice(h * SEGMENT_TOKENS, (h + 1) * SEGMENT_TOKENS)
                head = first + h
                o_ref[:, head * HEAD_SIZE : (head + 1) * HEAD_SIZE] = out[part]


def trunk_kernel(kv_heads, start_ref, q_ref, kt_ref, vt_ref, o_ref):
    rows = q_ref.shape[0]
    key_count = kt_ref.shape[0]
    query_at = start_ref[0] + lax.broadcasted_iota(jnp.int32, (rows, key_count), 0)
    causal = query_at >= lax.broadcasted_iota(jnp.int32, (rows, key_count), 1)
    for j in range(kv_heads):
        keys = head_cols(kt_ref, j)
        values = with_ones(head_cols(vt_ref, j))
        for head in range(j * GROUP, (j + 1) * GROUP):
            scores = jnp.where(causal, scores_of(head_cols(q_ref, head), keys), MASKED)
            peak = jnp.max(scores, axis=1, keepdims=True)
            weights = jnp.exp2((scores - peak) * LOG2E_SCALE).astype(jnp.bfloat16)
            summed = jnp.dot(weights, values, preferred_element_type=jnp.float32)
            o_ref[:, head * HEAD_SIZE : (head + 1) * HEAD_SIZE] = (
                summed[:, :HEAD_SIZE] / summed[:, HEAD_SIZE:]
            ).astype(jnp.bfloat16)


VMEM_LIMIT = 48 * 1024 * 1024


def near_call(tree_query, key_all, value_all, tree_key, tree_value):
    tokens, width = tree_query.shape
    slots = tokens // SEGMENT_TOKENS
    kv_width = tree_key.shape[1]
    kv_heads = kv_width // HEAD_SIZE
    trunk = key_all.shape[0]
    keys = trunk + SEGMENT_TOKENS
    whole = pl.BlockSpec((trunk, kv_width), lambda s: (0, 0))
    own = pl.BlockSpec((SEGMENT_TOKENS, kv_width), lambda s: (s, 0))
    wide = pl.BlockSpec((SEGMENT_TOKENS, width), lambda s: (s, 0))
    return pl.pallas_call(
        functools.partial(near_kernel, kv_heads),
        grid=(slots,),
        in_specs=[wide, whole, whole, own, own],
        out_specs=[wide, pl.BlockSpec((SEGMENT_TOKENS, STAT_WIDTH), lambda s: (s, 0))],
        out_shape=[
            jax.ShapeDtypeStruct((tokens, width), jnp.bfloat16),
            jax.ShapeDtypeStruct((tokens, STAT_WIDTH), jnp.float32),
        ],
        compiler_params=pltpu.CompilerParams(vmem_limit_bytes=VMEM_LIMIT),
        cost_estimate=pl.CostEstimate(
            flops=4 * tokens * width * keys,
            bytes_accessed=4 * tokens * width,
            transcendentals=tokens * width // HEAD_SIZE * keys,
        ),
        name="near",
    )(tree_query, key_all, value_all, tree_key, tree_value)


def far_call(places, seen, tree_query, near, stats, gathered, first_kv, earlier):
    tokens, width = tree_query.shape
    slots = tokens // SEGMENT_TOKENS
    kv_width = gathered.shape[2]
    kv_count = kv_width // HEAD_SIZE // 2
    share = kv_count * GROUP * HEAD_SIZE
    column = first_kv // kv_count
    wide = pl.BlockSpec((SEGMENT_TOKENS, share), lambda s, p, v: (s, column))
    in_specs = [
        wide,
        wide,
        pl.BlockSpec((SEGMENT_TOKENS, STAT_WIDTH), lambda s, p, v: (s, 0)),
        pl.BlockSpec((1, SEGMENT_TOKENS, kv_width), lambda s, p, v: (p[2 * s], 0, 0)),
        pl.BlockSpec((1, SEGMENT_TOKENS, kv_width), lambda s, p, v: (p[2 * s + 1], 0, 0)),
    ]
    operands = [places, seen, tree_query, near, stats, gathered, gathered]
    aliases = {}
    if earlier is not None:
        aliases = {len(operands): 0}
        in_specs.append(pl.BlockSpec(memory_space=pl.ANY))
        operands.append(earlier)
    return pl.pallas_call(
        functools.partial(far_kernel, first_kv, kv_count),
        grid_spec=pltpu.PrefetchScalarGridSpec(
            num_scalar_prefetch=2, grid=(slots,), in_specs=in_specs, out_specs=wide
        ),
        out_shape=jax.ShapeDtypeStruct((tokens, width), jnp.bfloat16),
        input_output_aliases=aliases,
        compiler_params=pltpu.CompilerParams(vmem_limit_bytes=VMEM_LIMIT),
        cost_estimate=pl.CostEstimate(
            flops=8 * tokens * share * SEGMENT_TOKENS,
            bytes_accessed=6 * tokens * share,
            transcendentals=tokens * share * 2,
        ),
        name="far",
    )(*operands)


def trunk_call(start, trunk_query, key_all, value_all):
    rows, width = trunk_query.shape
    kv_heads = key_all.shape[1] // HEAD_SIZE
    vmem = pl.BlockSpec(memory_space=pltpu.VMEM)
    return pl.pallas_call(
        functools.partial(trunk_kernel, kv_heads),
        in_specs=[pl.BlockSpec(memory_space=pltpu.SMEM), vmem, vmem, vmem],
        out_specs=vmem,
        out_shape=jax.ShapeDtypeStruct((rows, width), jnp.bfloat16),
        compiler_params=pltpu.CompilerParams(vmem_limit_bytes=VMEM_LIMIT),
        cost_estimate=pl.CostEstimate(
            flops=4 * rows * width * key_all.shape[0],
            bytes_accessed=4 * rows * width,
            transcendentals=rows * width // HEAD_SIZE * key_all.shape[0],
        ),
        name="trunk",
    )(start, trunk_query, key_all, value_all)


def local(
    trunk_query,
    trunk_key,
    trunk_value,
    tree_query,
    tree_key,
    tree_value,
    ancestors,
):
    me = lax.axis_index("ctx")
    kv_width = trunk_key.shape[1]
    slots = tree_query.shape[0] // SEGMENT_TOKENS
    total = ancestors.shape[0]
    sent = slots * 4 // 5

    slot_ids = jnp.arange(total, dtype=jnp.int32)
    inner = jnp.any(ancestors.reshape(-1, 1) == slot_ids[None, :], axis=0)
    earlier = (slot_ids[None, :] < slot_ids[:, None]) & (
        slot_ids[None, :] // slots == slot_ids[:, None] // slots
    )
    rank = jnp.sum(jnp.where(earlier & inner[None, :], 1, 0), axis=1)
    place = slot_ids // slots * sent + rank
    own_place = me * sent + jnp.arange(sent, dtype=jnp.int32)
    hit = inner[None, :] & (place[None, :] == own_place[:, None])
    picked = jnp.sum(jnp.where(hit, slot_ids[None, :] % slots, 0), axis=1)

    own_lists = lax.dynamic_slice_in_dim(ancestors, me * slots, slots, 0).reshape(-1)
    seen = (own_lists >= 0).astype(jnp.int32)
    places = jnp.sum(
        jnp.where(own_lists[:, None] == slot_ids[None, :], place[None, :], 0), axis=1
    )

    trunk_both = lax.all_gather(
        jnp.concatenate([trunk_key, trunk_value], axis=1), "ctx", axis=0, tiled=True
    )
    key_all, value_all = trunk_both[:, :kv_width], trunk_both[:, kv_width:]
    own_keys = tree_key.reshape(slots, SEGMENT_TOKENS, kv_width)[picked]
    own_values = tree_value.reshape(slots, SEGMENT_TOKENS, kv_width)[picked]
    kv_heads = kv_width // HEAD_SIZE
    cuts = [0, kv_heads - 1, kv_heads] if kv_heads > 1 else [0, kv_heads]
    gathered = []
    for first, last in zip(cuts[:-1], cuts[1:]):
        cols = slice(first * HEAD_SIZE, last * HEAD_SIZE)
        packed = jnp.concatenate([own_keys[:, :, cols], own_values[:, :, cols]], axis=2)
        gathered.append(lax.all_gather(packed, "ctx", axis=0, tiled=True))

    near, stats = near_call(tree_query, key_all, value_all, tree_key, tree_value)
    start = (me * trunk_query.shape[0]).astype(jnp.int32).reshape(1)
    trunk_out = trunk_call(start, trunk_query, key_all, value_all)
    tree_out = None
    for first, pieces in zip(cuts[:-1], gathered):
        tree_out = far_call(places, seen, tree_query, near, stats, pieces, first, tree_out)
    return trunk_out, tree_out


def solution(mesh):
    split = P(("rep", "ctx"), "head")
    return jax.shard_map(
        local,
        mesh=mesh,
        in_specs=(split,) * 6 + (P("rep", None),),
        out_specs=(split, split),
        check_vma=False,
    )
```

```python
import functools
import math

import jax
import jax.numpy as jnp
from jax import lax
from jax.experimental import pallas as pl
from jax.experimental.pallas import tpu as pltpu
from jax.sharding import PartitionSpec as P

HEAD_SIZE = 128
SEGMENT_TOKENS = 128
GROUP = 8
ROW_HEADS = 2
FAR_HEADS = 4
STAT_WIDTH = 128
MASKED = -1e30
LOG2E_SCALE = math.log2(math.e) / math.sqrt(HEAD_SIZE)


def stack_heads(ref, first, count):
    blocks = [
        ref[:, (first + h) * HEAD_SIZE : (first + h + 1) * HEAD_SIZE] for h in range(count)
    ]
    return jnp.concatenate(blocks, axis=0)


def scores_of(queries, key_rows):
    return lax.dot_general(
        queries, key_rows, (((1,), (1,)), ((), ())), preferred_element_type=jnp.float32
    )


def with_ones(value_rows):
    return jnp.concatenate([value_rows, jnp.ones_like(value_rows)], axis=1)


def head_cols(ref, j):
    return ref[:, j * HEAD_SIZE : (j + 1) * HEAD_SIZE]


def near_kernel(kv_heads, q_ref, kt_ref, vt_ref, ks_ref, vs_ref, o_ref, stat_ref):
    rows = ROW_HEADS * SEGMENT_TOKENS
    lane = lax.broadcasted_iota(jnp.int32, (SEGMENT_TOKENS, STAT_WIDTH), 1)
    query_at = lax.broadcasted_iota(jnp.int32, (rows, SEGMENT_TOKENS), 0) % SEGMENT_TOKENS
    key_at = lax.broadcasted_iota(jnp.int32, (rows, SEGMENT_TOKENS), 1)
    causal = query_at >= key_at
    stats = jnp.zeros((SEGMENT_TOKENS, STAT_WIDTH), jnp.float32)
    for j in range(kv_heads):
        trunk_keys, self_keys = head_cols(kt_ref, j), head_cols(ks_ref, j)
        trunk_values = with_ones(head_cols(vt_ref, j))
        self_values = with_ones(head_cols(vs_ref, j))
        for first in range(j * GROUP, (j + 1) * GROUP, ROW_HEADS):
            queries = stack_heads(q_ref, first, ROW_HEADS)
            trunk_scores = scores_of(queries, trunk_keys)
            self_scores = jnp.where(causal, scores_of(queries, self_keys), MASKED)
            peak = jnp.maximum(
                jnp.max(trunk_scores, axis=1, keepdims=True),
                jnp.max(self_scores, axis=1, keepdims=True),
            )
            trunk_weights = jnp.exp2((trunk_scores - peak) * LOG2E_SCALE).astype(jnp.bfloat16)
            self_weights = jnp.exp2((self_scores - peak) * LOG2E_SCALE).astype(jnp.bfloat16)
            summed = jnp.dot(
                trunk_weights, trunk_values, preferred_element_type=jnp.float32
            ) + jnp.dot(self_weights, self_values, preferred_element_type=jnp.float32)
            for h in range(ROW_HEADS):
                part = slice(h * SEGMENT_TOKENS, (h + 1) * SEGMENT_TOKENS)
                head = first + h
                total = summed[part, HEAD_SIZE:]
                o_ref[:, head * HEAD_SIZE : (head + 1) * HEAD_SIZE] = (
                    summed[part, :HEAD_SIZE] / total
                ).astype(jnp.bfloat16)
                level = peak[part] * LOG2E_SCALE + jnp.log2(total)
                stats = jnp.where(lane == head, level, stats)
    stat_ref[...] = stats


def far_kernel(
    first_kv,
    kv_count,
    place_ref,
    seen_ref,
    q_ref,
    near_ref,
    stat_ref,
    kv0_ref,
    kv1_ref,
    *rest,
):
    o_ref = rest[-1]
    step = pl.program_id(0)
    bars = [
        jnp.where(seen_ref[2 * step + n] > 0, 0.0, MASKED).astype(jnp.float32) for n in range(2)
    ]
    key_at = lax.broadcasted_iota(jnp.int32, (1, 2 * SEGMENT_TOKENS), 1)
    bar = jnp.where(key_at < SEGMENT_TOKENS, bars[0], bars[1])
    width = kv_count * HEAD_SIZE
    for j in range(kv_count):
        cols = slice(j * HEAD_SIZE, (j + 1) * HEAD_SIZE)
        vcols = slice(width + j * HEAD_SIZE, width + (j + 1) * HEAD_SIZE)
        keys = jnp.concatenate([kv0_ref[0, :, cols], kv1_ref[0, :, cols]], axis=0)
        values = with_ones(jnp.concatenate([kv0_ref[0, :, vcols], kv1_ref[0, :, vcols]], axis=0))
        for first in range(j * GROUP, (j + 1) * GROUP, FAR_HEADS):
            queries = stack_heads(q_ref, first, FAR_HEADS)
            scores = scores_of(queries, keys) * LOG2E_SCALE + bar
            stat = first_kv * GROUP + first
            level = jnp.concatenate(
                [stat_ref[:, stat + h : stat + h + 1] for h in range(FAR_HEADS)], axis=0
            )
            peak = jnp.maximum(level, jnp.max(scores, axis=1, keepdims=True))
            weights = jnp.exp2(scores - peak).astype(jnp.bfloat16)
            summed = jnp.dot(weights, values, preferred_element_type=jnp.float32)
            factor = jnp.exp2(level - peak)
            near = stack_heads(near_ref, first, FAR_HEADS).astype(jnp.float32)
            total = factor + summed[:, HEAD_SIZE:]
            out = ((factor * near + summed[:, :HEAD_SIZE]) / total).astype(jnp.bfloat16)
            for h in range(FAR_HEADS):
                part = slice(h * SEGMENT_TOKENS, (h + 1) * SEGMENT_TOKENS)
                head = first + h
                o_ref[:, head * HEAD_SIZE : (head + 1) * HEAD_SIZE] = out[part]


def trunk_kernel(kv_heads, start_ref, q_ref, kt_ref, vt_ref, o_ref):
    rows = q_ref.shape[0]
    key_count = kt_ref.shape[0]
    query_at = start_ref[0] + lax.broadcasted_iota(jnp.int32, (rows, key_count), 0)
    causal = query_at >= lax.broadcasted_iota(jnp.int32, (rows, key_count), 1)
    for j in range(kv_heads):
        keys = head_cols(kt_ref, j)
        values = with_ones(head_cols(vt_ref, j))
        for head in range(j * GROUP, (j + 1) * GROUP):
            scores = jnp.where(causal, scores_of(head_cols(q_ref, head), keys), MASKED)
            peak = jnp.max(scores, axis=1, keepdims=True)
            weights = jnp.exp2((scores - peak) * LOG2E_SCALE).astype(jnp.bfloat16)
            summed = jnp.dot(weights, values, preferred_element_type=jnp.float32)
            o_ref[:, head * HEAD_SIZE : (head + 1) * HEAD_SIZE] = (
                summed[:, :HEAD_SIZE] / summed[:, HEAD_SIZE:]
            ).astype(jnp.bfloat16)


VMEM_LIMIT = 48 * 1024 * 1024


def near_call(tree_query, key_all, value_all, tree_key, tree_value):
    tokens, width = tree_query.shape
    slots = tokens // SEGMENT_TOKENS
    kv_width = tree_key.shape[1]
    kv_heads = kv_width // HEAD_SIZE
    trunk = key_all.shape[0]
    keys = trunk + SEGMENT_TOKENS
    whole = pl.BlockSpec((trunk, kv_width), lambda s: (0, 0))
    own = pl.BlockSpec((SEGMENT_TOKENS, kv_width), lambda s: (s, 0))
    wide = pl.BlockSpec((SEGMENT_TOKENS, width), lambda s: (s, 0))
    return pl.pallas_call(
        functools.partial(near_kernel, kv_heads),
        grid=(slots,),
        in_specs=[wide, whole, whole, own, own],
        out_specs=[wide, pl.BlockSpec((SEGMENT_TOKENS, STAT_WIDTH), lambda s: (s, 0))],
        out_shape=[
            jax.ShapeDtypeStruct((tokens, width), jnp.bfloat16),
            jax.ShapeDtypeStruct((tokens, STAT_WIDTH), jnp.float32),
        ],
        compiler_params=pltpu.CompilerParams(vmem_limit_bytes=VMEM_LIMIT),
        cost_estimate=pl.CostEstimate(
            flops=4 * tokens * width * keys,
            bytes_accessed=4 * tokens * width,
            transcendentals=tokens * width // HEAD_SIZE * keys,
        ),
        name="near",
    )(tree_query, key_all, value_all, tree_key, tree_value)


def far_call(places, seen, tree_query, near, stats, gathered, first_kv, earlier):
    tokens, width = tree_query.shape
    slots = tokens // SEGMENT_TOKENS
    kv_width = gathered.shape[2]
    kv_count = kv_width // HEAD_SIZE // 2
    share = kv_count * GROUP * HEAD_SIZE
    column = first_kv // kv_count
    wide = pl.BlockSpec((SEGMENT_TOKENS, share), lambda s, p, v: (s, column))
    in_specs = [
        wide,
        wide,
        pl.BlockSpec((SEGMENT_TOKENS, STAT_WIDTH), lambda s, p, v: (s, 0)),
        pl.BlockSpec((1, SEGMENT_TOKENS, kv_width), lambda s, p, v: (p[2 * s], 0, 0)),
        pl.BlockSpec((1, SEGMENT_TOKENS, kv_width), lambda s, p, v: (p[2 * s + 1], 0, 0)),
    ]
    operands = [places, seen, tree_query, near, stats, gathered, gathered]
    aliases = {}
    if earlier is not None:
        aliases = {len(operands): 0}
        in_specs.append(pl.BlockSpec(memory_space=pl.ANY))
        operands.append(earlier)
    return pl.pallas_call(
        functools.partial(far_kernel, first_kv, kv_count),
        grid_spec=pltpu.PrefetchScalarGridSpec(
            num_scalar_prefetch=2, grid=(slots,), in_specs=in_specs, out_specs=wide
        ),
        out_shape=jax.ShapeDtypeStruct((tokens, width), jnp.bfloat16),
        input_output_aliases=aliases,
        compiler_params=pltpu.CompilerParams(vmem_limit_bytes=VMEM_LIMIT),
        cost_estimate=pl.CostEstimate(
            flops=8 * tokens * share * SEGMENT_TOKENS,
            bytes_accessed=6 * tokens * share,
            transcendentals=tokens * share * 2,
        ),
        name="far",
    )(*operands)


def trunk_call(start, trunk_query, key_all, value_all):
    rows, width = trunk_query.shape
    kv_heads = key_all.shape[1] // HEAD_SIZE
    vmem = pl.BlockSpec(memory_space=pltpu.VMEM)
    return pl.pallas_call(
        functools.partial(trunk_kernel, kv_heads),
        in_specs=[pl.BlockSpec(memory_space=pltpu.SMEM), vmem, vmem, vmem],
        out_specs=vmem,
        out_shape=jax.ShapeDtypeStruct((rows, width), jnp.bfloat16),
        compiler_params=pltpu.CompilerParams(vmem_limit_bytes=VMEM_LIMIT),
        cost_estimate=pl.CostEstimate(
            flops=4 * rows * width * key_all.shape[0],
            bytes_accessed=4 * rows * width,
            transcendentals=rows * width // HEAD_SIZE * key_all.shape[0],
        ),
        name="trunk",
    )(start, trunk_query, key_all, value_all)


def local(
    trunk_query,
    trunk_key,
    trunk_value,
    tree_query,
    tree_key,
    tree_value,
    ancestors,
):
    me = lax.axis_index("ctx")
    kv_width = trunk_key.shape[1]
    slots = tree_query.shape[0] // SEGMENT_TOKENS
    total = ancestors.shape[0]
    sent = slots * 4 // 5

    slot_ids = jnp.arange(total, dtype=jnp.int32)
    inner = jnp.any(ancestors.reshape(-1, 1) == slot_ids[None, :], axis=0)
    earlier = (slot_ids[None, :] < slot_ids[:, None]) & (
        slot_ids[None, :] // slots == slot_ids[:, None] // slots
    )
    rank = jnp.sum(jnp.where(earlier & inner[None, :], 1, 0), axis=1)
    place = slot_ids // slots * sent + rank
    own_place = me * sent + jnp.arange(sent, dtype=jnp.int32)
    hit = inner[None, :] & (place[None, :] == own_place[:, None])
    picked = jnp.sum(jnp.where(hit, slot_ids[None, :] % slots, 0), axis=1)

    own_lists = lax.dynamic_slice_in_dim(ancestors, me * slots, slots, 0).reshape(-1)
    seen = (own_lists >= 0).astype(jnp.int32)
    places = jnp.sum(
        jnp.where(own_lists[:, None] == slot_ids[None, :], place[None, :], 0), axis=1
    )

    trunk_both = lax.all_gather(
        jnp.concatenate([trunk_key, trunk_value], axis=1), "ctx", axis=0, tiled=True
    )
    key_all, value_all = trunk_both[:, :kv_width], trunk_both[:, kv_width:]
    own_keys = tree_key.reshape(slots, SEGMENT_TOKENS, kv_width)[picked]
    own_values = tree_value.reshape(slots, SEGMENT_TOKENS, kv_width)[picked]
    kv_heads = kv_width // HEAD_SIZE
    cuts = [0, kv_heads - 1, kv_heads] if kv_heads > 1 else [0, kv_heads]
    gathered = []
    for first, last in zip(cuts[:-1], cuts[1:]):
        cols = slice(first * HEAD_SIZE, last * HEAD_SIZE)
        packed = jnp.concatenate([own_keys[:, :, cols], own_values[:, :, cols]], axis=2)
        gathered.append(lax.all_gather(packed, "ctx", axis=0, tiled=True))

    near, stats = near_call(tree_query, key_all, value_all, tree_key, tree_value)
    start = (me * trunk_query.shape[0]).astype(jnp.int32).reshape(1)
    trunk_out = trunk_call(start, trunk_query, key_all, value_all)
    tree_out = None
    for first, pieces in zip(cuts[:-1], gathered):
        tree_out = far_call(places, seen, tree_query, near, stats, pieces, first, tree_out)
    return trunk_out, tree_out


def solution(mesh):
    split = P(("rep", "ctx"), "head")
    return jax.shard_map(
        local,
        mesh=mesh,
        in_specs=(split,) * 6 + (P("rep", None),),
        out_specs=(split, split),
        check_vma=False,
    )
```
